32 devices in a mesh: dp: 8 (over y, x, core), inv: 4 (over z).
Axes of the slice: x: 2, y: 2, z: 4, core: 2. Of those that a mesh axis runs over, the one named last changes fastest.
Arguments:
- acts: bfloat16 [1024, 6144], P('dp', 'inv'), may hold values from -6 to 6
- grads_out: bfloat16 [1024, 24576], P('inv', 'dp'), may hold values from -0.119628906 to 0.119628906
- scale_exp: int32 [1024], replicated, may hold values from 0 to 3
- shard_tokens: int32 [8], replicated, may hold values from 1 to 128, 768 in all
Outputs:
- precond: bfloat16 [6144, 24576], P('inv', 'dp')
The draws below stay inside these ranges and needn't reach their ends.
Inputs may be any that keep to these rules, and one draw needn't show every extreme that they name: `shard_tokens`: largest entry is exactly 128; entries sum to 768.
All inputs are finite; a program needn't handle non-finite values.
Results may differ from the reference program's by a relative error of at most 0.0015.
Values may be sent and summed in bfloat16 or wider, within the bound.
A program may use at most 64 MiB of HBM per device.

```python
import math
import jax
import jax.numpy as jnp
import numpy as np
from jax import lax

D = 6144
FF = 24576
BLK = 128
ITERS = 8
TOK_DEV = 128
TOKENS = 1024
VALID = 768
N_DP = 8


def set_ends(result, stream_key, least, high):
    longest = result.shape.index(max(result.shape))
    spots = []
    for shift in (0, 1):
        where = [jax.random.randint(jax.random.fold_in(stream_key, axis), (), 0, length) for axis, length in enumerate(result.shape)]
        where[longest] = (where[longest] + shift) % result.shape[longest]
        spots.append(tuple(where))
    return result.at[spots[0]].set(least).at[spots[1]].set(high)


def block_levels(rng, shape, split, low, largest):
    def one(axis_at, shards_of):
        steps = jax.random.uniform(jax.random.fold_in(jax.random.fold_in(rng, 6), axis_at), (shards_of,), jnp.float32, low / len(split), largest / len(split))
        return jnp.repeat(jnp.exp(steps), shape[axis_at] // shards_of).reshape((-1,) + (1,) * (len(shape) - axis_at - 1))

    factor_of = one(*split[0])
    for cut in split[1:]:
        factor_of = factor_of * one(*cut)
    return factor_of


def profile(count, total, most, skew):
    loads = [(1 << 20) // math.isqrt(rank ** skew) + 1 for rank in range(2, count + 1)]
    surplus, holding = total - most - (count - 1), [1] * (count - 1)
    while surplus > 0:
        free = [i for i in range(count - 1) if holding[i] < most]
        whole, remaining = sum([loads[i] for i in free]), surplus
        for i in free:
            extra = min(most - holding[i], max(1, remaining * loads[i] // whole), surplus)
            holding[i] = holding[i] + extra
            surplus = surplus - extra
    return np.array([most] + holding)


def uneven(stream_key, amount, total, reach, slope):
    if amount == 2:
        one = jax.random.randint(stream_key, (), max(1, total - reach), min(reach, total - 1) + 1)
        return jnp.stack([one, total - one])
    tallies = jnp.asarray(profile(amount, total, reach, slope), jnp.int32)
    twos = (amount - 1) // 2
    giver, receiver = tallies[1:1 + 2 * twos:2], tallies[2:2 + 2 * twos:2]
    slack = jnp.minimum(giver - 1, reach - receiver)
    passed = jax.random.randint(jax.random.fold_in(stream_key, 1), (twos,), 0, 1 << 20) % (slack + 1)
    tallies = tallies.at[1:1 + 2 * twos:2].set(giver - passed).at[2:2 + 2 * twos:2].set(receiver + passed)
    return tallies[jax.random.permutation(jax.random.fold_in(stream_key, 2), amount)]


def scatter_about(rng, dims, deviation, most, cuts=(), held_as=jnp.bfloat16):
    array = deviation * jax.random.normal(rng, dims, jnp.float32)
    if cuts:
        array = array * block_levels(rng, dims, cuts, -0.22, 0.18)
    return jnp.clip(array, -most, most).astype(held_as)


def setup_inputs(seed: int = 0) -> dict:
    arg_keys = jax.random.split(jax.random.key(seed), 5)
    acts = scatter_about(arg_keys[0], (TOKENS, D), 1.0, 6.0, ((0, 8), (1, 4)))
    grads_out = scatter_about(arg_keys[1], (TOKENS, FF), 0.02, 0.119628906, ((0, 4), (1, 8)))
    scale_exp = set_ends(jax.random.randint(arg_keys[2], (TOKENS,), 0, 4), jax.random.fold_in(arg_keys[2], 1), 0, 3).astype(jnp.int32)
    shard_tokens = uneven(arg_keys[3], N_DP, VALID, TOK_DEV, 2).astype(jnp.int32)
    return {"acts": acts, "grads_out": grads_out, "scale_exp": scale_exp, "shard_tokens": shard_tokens}


damping = 1e-3


def block_cov(rows, order):
    shaped = rows.astype(jnp.float32).reshape(rows.shape[0], rows.shape[1] // order, order)
    return jnp.einsum('tbi,tbj->bij', shaped, shaped, precision=lax.Precision.HIGHEST)


def damped(cov):
    order = cov.shape[-1]
    eye = jnp.eye(order, dtype=jnp.float32)
    trace = jnp.trace(cov, axis1=1, axis2=2)
    return cov + damping * (trace / order)[:, None, None] * eye


def newton(matrix):
    order = matrix.shape[-1]
    eye = jnp.eye(order, dtype=jnp.float32)
    trace = jnp.trace(matrix, axis1=1, axis2=2)
    approx = eye[None] / trace[:, None, None]
    for step in range(ITERS):
        inner = jnp.einsum('bij,bjk->bik', matrix, approx, precision=lax.Precision.HIGHEST)
        approx = jnp.einsum('bij,bjk->bik', approx, 2.0 * eye - inner, precision=lax.Precision.HIGHEST)
    return approx


def reference(acts, grads_out, scale_exp, shard_tokens):
    tokens = acts.shape[0]
    ids = jnp.arange(tokens, dtype=jnp.int32)
    limit = jnp.repeat(shard_tokens, TOK_DEV)
    live = ids % TOK_DEV < limit
    row_weight = jnp.where(live, jnp.exp2(-scale_exp.astype(jnp.float32)), 0.0)
    masked = acts * live.astype(jnp.bfloat16)[:, None]
    scaled = grads_out * row_weight.astype(jnp.bfloat16)[:, None]
    count = jnp.sum(shard_tokens).astype(jnp.float32)
    grad = jnp.dot(masked.T, scaled, preferred_element_type=jnp.float32) / count
    a_inv = newton(damped(block_cov(masked, BLK) / count))
    g_inv = newton(damped(block_cov(scaled, BLK) / count))
    shaped = grad.reshape(D // BLK, BLK, FF // BLK, BLK)
    left = jnp.einsum('bij,bjck->bick', a_inv, shaped, precision=lax.Precision.HIGHEST)
    both = jnp.einsum('bick,ckl->bicl', left, g_inv, precision=lax.Precision.HIGHEST)
    return both.reshape(D, FF).astype(jnp.bfloat16)
```

```python
import functools

import jax
import jax.numpy as jnp
from jax import lax
from jax.experimental import pallas as pl
from jax.experimental.pallas import tpu as pltpu
from jax.sharding import PartitionSpec as P

BLK = 128
ITERS = 8
TOK_DEV = 128
WIDTH = 256
AHEAD = 4
DAMPING = 0.001
MESH = pl.DeviceIdType.MESH
f32, bf16 = jnp.float32, jnp.bfloat16


def dot(a, b, dims=((1,), (0,))):
    return lax.dot_general(a, b, (dims, ((), ())), preferred_element_type=f32)


def split(x):
    hi = x.astype(bf16)
    return hi, (x - hi.astype(f32)).astype(bf16)


def pairs(hi, lo):
    row = jnp.concatenate([hi, lo], axis=1)
    return row, jnp.concatenate([row, row], axis=0)


def halves(r):
    return r[:, :BLK] + r[:, BLK:]


def newton(covs):
    i = lax.broadcasted_iota(jnp.int32, (BLK, BLK), 0)
    j = lax.broadcasted_iota(jnp.int32, (BLK, BLK), 1)
    diag = i == j
    ts, xs, invs = [], [], []
    for c in covs:
        tr = jnp.sum(jnp.where(diag, c, 0.0), keepdims=True)
        m = c + jnp.where(diag, DAMPING * (tr / BLK), 0.0)
        inv = 1.0 / jnp.sum(jnp.where(diag, m, 0.0), keepdims=True)
        t = m * inv
        ts.append(t)
        xs.append(jnp.where(diag, 2.0, 0.0) - t)
        invs.append(inv)
    for step in range(ITERS):
        for b in range(len(covs)):
            t, x = ts[b], xs[b]
            t_row, t_mat = pairs(*split(t))
            if step == 0:
                ts[b] = 2.0 * t - halves(dot(t_row, t_mat))
                continue
            x_row = jnp.concatenate(split(x), axis=1)
            if step == ITERS - 1:
                xs[b] = 2.0 * x - halves(dot(x_row, t_mat))
                continue
            r = halves(dot(jnp.concatenate([t_row, x_row], axis=0), t_mat))
            ts[b] = 2.0 * t - r[:BLK]
            xs[b] = 2.0 * x - r[BLK:]
    return [x * inv for x, inv in zip(xs, invs)]


def kernel(n_dp, n_inv, cap, acts_t, grads, pos_col, pos_row, w_row, count, out,
           acts_all, place, pa, fl, fr, own, stage,
           a_send, a_recv, l_send, l_recv, r_send, r_recv, o_sem):
    dp = lax.axis_index("dp")
    z = lax.axis_index("inv")
    units = acts_t.shape[0]
    tp = grads.shape[0]
    chunks, live, width = own.shape
    tokens = pos_col.shape[0]

    barrier = pltpu.get_barrier_semaphore()

    def greet(d, _):
        pl.semaphore_signal(barrier, inc=1, device_id={"dp": lax.rem(dp + d, n_dp)}, device_id_type=MESH)
        return 0

    lax.fori_loop(1, n_dp, greet, 0)

    @pl.when(z > 0)
    def _():
        pl.semaphore_signal(barrier, inc=1, device_id={"inv": z - 1}, device_id_type=MESH)

    @pl.when(z < n_inv - 1)
    def _():
        pl.semaphore_signal(barrier, inc=1, device_id={"inv": z + 1}, device_id_type=MESH)

    at_end = (z == 0) | (z == n_inv - 1)

    @pl.when(at_end)
    def _():
        pl.semaphore_wait(barrier, n_dp)

    @pl.when(jnp.logical_not(at_end))
    def _():
        pl.semaphore_wait(barrier, n_dp + 1)

    def acts_copy(owner, peer):
        cols = pl.ds(pl.multiple_of(owner * TOK_DEV, TOK_DEV), TOK_DEV)
        return pltpu.make_async_remote_copy(
            src_ref=acts_t, dst_ref=acts_all.at[:, cols], send_sem=a_send.at[peer], recv_sem=a_recv.at[owner],
            device_id={"dp": peer}, device_id_type=MESH)

    def send_acts(d, _):
        acts_copy(dp, lax.rem(dp + d, n_dp)).start()
        return 0

    lax.fori_loop(1, n_dp, send_acts, 0)

    def wait_acts(d, _):
        peer = lax.rem(dp + d, n_dp)
        acts_copy(peer, peer).wait_recv()
        return 0

    def wait_acts_sent(d, _):
        acts_copy(dp, lax.rem(dp + d, n_dp)).wait_send()
        return 0

    hops = min(-(-cap // tp), n_inv - 1)
    left_rows = []
    right_rows = []
    for k in range(hops):
        hi = live - k * tp
        lo = max(live - cap, hi - tp)
        left_rows.append((lo, hi - lo))
        right_rows.append((k * tp, min(cap, (k + 1) * tp) - k * tp))

    def left_copy(c, k):
        lo, size = left_rows[k]
        part = fr.at[c, pl.ds(lo, size), :]
        return pltpu.make_async_remote_copy(
            src_ref=part, dst_ref=part, send_sem=l_send.at[k, c], recv_sem=l_recv.at[k, c],
            device_id={"inv": lax.max(z - 1, 0)}, device_id_type=MESH)

    def right_copy(c, k):
        lo, size = right_rows[k]
        part = fl.at[c, pl.ds(lo, size), :]
        return pltpu.make_async_remote_copy(
            src_ref=part, dst_ref=part, send_sem=r_send.at[k, c], recv_sem=r_recv.at[k, c],
            device_id={"inv": lax.min(z + 1, n_inv - 1)}, device_id_type=MESH)

    def leftward(c):
        if cap < live:
            fr[c, :live - cap, :] = own[c, :live - cap, :]
        for k in range(hops):
            lo, size = left_rows[k]
            rows = pl.ds(lo, size)

            @pl.when(z < n_inv - 1 - k)
            def _():
                left_copy(c, k).wait_recv()
                fr[c, rows, :] = fr[c, rows, :] + own[c, rows, :]

            @pl.when(z >= n_inv - 1 - k)
            def _():
                fr[c, rows, :] = own[c, rows, :]

            @pl.when((z > 0) & (z < n_inv - k))
            def _():
                left_copy(c, k).start()

    def rightward(c):
        if cap < live:
            fl[c, cap:, :] = own[c, cap:, :]
        for k in range(hops):
            lo, size = right_rows[k]
            rows = pl.ds(lo, size)

            @pl.when(z > k)
            def _():
                right_copy(c, k).wait_recv()
                fl[c, rows, :] = fl[c, rows, :] + own[c, rows, :]

            @pl.when(z <= k)
            def _():
                fl[c, rows, :] = own[c, rows, :]

            @pl.when((z < n_inv - 1) & (z >= k))
            def _():
                right_copy(c, k).start()

    slot = lax.broadcasted_iota(jnp.int32, (live, tp), 0)
    place_own = jnp.where(slot == pos_row[...], w_row[...], 0.0).astype(bf16)

    def relay(c, _):
        cols = pl.ds(pl.multiple_of(c * width, width), width)
        own[c] = dot(place_own, grads[:, cols]).astype(bf16)

        @pl.when(z >= n_inv // 2)
        def _():
            leftward(c)

        rightward(c)

        @pl.when(z < n_inv // 2)
        def _():
            leftward(c)

        both = fr[c].astype(f32) + fl[c].astype(f32)
        own[c] = (both - own[c].astype(f32)).astype(bf16)
        return 0

    ahead = min(AHEAD, chunks)
    lax.fori_loop(0, ahead, relay, 0)

    def fill(s, _):
        rows = pl.ds(pl.multiple_of(s * TOK_DEV, TOK_DEV), TOK_DEV)
        spot = lax.broadcasted_iota(jnp.int32, (TOK_DEV, live), 1)
        place[rows, :] = jnp.where(spot == pos_col[rows, :], 1.0, 0.0).astype(bf16)
        return 0

    lax.fori_loop(0, tokens // TOK_DEV, fill, 0)
    acts_all[:, pl.ds(pl.multiple_of(dp * TOK_DEV, TOK_DEV), TOK_DEV)] = acts_t[...]
    lax.fori_loop(1, n_dp, wait_acts, 0)

    a_blocks = units // BLK
    group = max(g for g in (1, 2, 3, 4) if a_blocks % g == 0)

    def input_side(g, _):
        rows = [pl.ds(pl.multiple_of((g * group + i) * BLK, BLK), BLK) for i in range(group)]
        masked = [dot(acts_all[r, :], place[...]).astype(bf16) for r in rows]
        covs = [dot(m, m, ((1,), (1,))) for m in masked]
        for r, m, x in zip(rows, masked, newton(covs)):
            x_row = jnp.concatenate(split(x * count[...]), axis=1)
            hi, lo = split(dot(x_row, jnp.concatenate([m, m], axis=0)))
            pa[r, :live] = hi
            pa[r, live:2 * live] = lo
            pa[r, 2 * live:] = hi
        return 0

    lax.fori_loop(0, a_blocks // group, input_side, 0)

    step_rows = 512 if units % 512 == 0 else units

    def out_copy(c):
        cols = pl.ds(pl.multiple_of(c * width, width), width)
        return pltpu.make_async_copy(stage.at[c], out.at[:, cols], o_sem.at[c])

    def finish(c):
        parts = [own[c, :, i * BLK:(i + 1) * BLK] for i in range(width // BLK)]
        covs = [dot(s, s, ((0,), (0,))) for s in parts]
        his, los = [], []
        for s, x in zip(parts, newton(covs)):
            hi, lo = split(halves(dot(s, jnp.concatenate(split(x), axis=1))))
            his.append(hi)
            los.append(lo)
        hi = jnp.concatenate(his, axis=1)
        q = jnp.concatenate([hi, hi, jnp.concatenate(los, axis=1)], axis=0)

        def rows_step(m, _):
            rows = pl.ds(pl.multiple_of(m * step_rows, step_rows), step_rows)
            stage[c, rows, :] = dot(pa[rows, :], q).astype(bf16)
            return 0

        lax.fori_loop(0, units // step_rows, rows_step, 0)
        out_copy(c).start()

    def main(c, _):
        @pl.when(c + ahead < chunks)
        def _():
            relay(c + ahead, 0)

        finish(c)
        return 0

    lax.fori_loop(0, chunks, main, 0)

    lax.fori_loop(1, n_dp, wait_acts_sent, 0)

    def drain(c, _):
        out_copy(c).wait()
        for k in range(hops):
            @pl.when((z > 0) & (z < n_inv - k))
            def _():
                left_copy(c, k).wait_send()

            @pl.when((z < n_inv - 1) & (z >= k))
            def _():
                right_copy(c, k).wait_send()
        return 0

    lax.fori_loop(0, chunks, drain, 0)


def call(n_dp, n_inv, cap, collective_id, acts_t, grads, pos_col, pos_row, w_row, count):
    units, tp, cols = acts_t.shape[0], grads.shape[0], grads.shape[1]
    tokens = pos_col.shape[0]
    live = tokens * 3 // 4
    chunks = cols // WIDTH
    hops = min(-(-cap // tp), n_inv - 1)
    vmem = pl.BlockSpec(memory_space=pltpu.VMEM)
    return pl.pallas_call(
        functools.partial(kernel, n_dp, n_inv, cap),
        out_shape=jax.ShapeDtypeStruct((units, cols), bf16),
        in_specs=[vmem] * 6,
        out_specs=pl.BlockSpec(memory_space=pl.ANY),
        scratch_shapes=[
            pltpu.VMEM((units, tokens), bf16),
            pltpu.VMEM((tokens, live), bf16),
            pltpu.VMEM((units, 3 * live), bf16),
            pltpu.VMEM((chunks, live, WIDTH), bf16),
            pltpu.VMEM((chunks, live, WIDTH), bf16),
            pltpu.VMEM((chunks, live, WIDTH), bf16),
            pltpu.VMEM((chunks, units, WIDTH), bf16),
            pltpu.SemaphoreType.DMA((n_dp,)),
            pltpu.SemaphoreType.DMA((n_dp,)),
            pltpu.SemaphoreType.DMA((hops, chunks)),
            pltpu.SemaphoreType.DMA((hops, chunks)),
            pltpu.SemaphoreType.DMA((hops, chunks)),
            pltpu.SemaphoreType.DMA((hops, chunks)),
            pltpu.SemaphoreType.DMA((chunks,)),
        ],
        compiler_params=pltpu.CompilerParams(
            collective_id=collective_id, has_side_effects=True, vmem_limit_bytes=60 * 2**20),
        cost_estimate=pl.CostEstimate(
            flops=6 * units * live * cols, bytes_accessed=4 * units * cols, transcendentals=0),
    )(acts_t, grads, pos_col, pos_row, w_row, count)


def local(n_dp, n_inv, acts, grads_out, scale_exp, shard_tokens):
    tp = grads_out.shape[0]
    tokens = acts.shape[0] * n_dp
    ids = jnp.arange(tokens, dtype=jnp.int32)
    in_shard = ids % TOK_DEV
    limit = jnp.repeat(shard_tokens, TOK_DEV)
    first = jnp.repeat(jnp.cumsum(shard_tokens) - shard_tokens, TOK_DEV)
    pos = jnp.where(in_shard < limit, first + in_shard, -1).astype(jnp.int32)
    weight = jnp.exp2(-scale_exp.astype(f32))
    start = lax.axis_index("inv") * tp
    pos_row = lax.dynamic_slice_in_dim(pos, start, tp)[None, :]
    w_row = lax.dynamic_slice_in_dim(weight, start, tp)[None, :]
    count = jnp.sum(shard_tokens).astype(f32).reshape(1, 1)
    live = tokens * 3 // 4
    return call(n_dp, n_inv, live, 0, acts.T, grads_out, pos[:, None], pos_row, w_row, count)


def solution(mesh):
    placed = (P("dp", "inv"), P("inv", "dp"), P(), P())
    return jax.shard_map(
        functools.partial(local, mesh.shape["dp"], mesh.shape["inv"]),
        mesh=mesh, in_specs=placed, out_specs=P("inv", "dp"), check_vma=False)
```

```python
import functools

import jax
import jax.numpy as jnp
from jax import lax
from jax.experimental import pallas as pl
from jax.experimental.pallas import tpu as pltpu
from jax.sharding import PartitionSpec as P

BLK = 128
ITERS = 8
TOK_DEV = 128
WIDTH = 256
DAMPING = 0.001
MESH = pl.DeviceIdType.MESH
f32, bf16 = jnp.float32, jnp.bfloat16


def dot(a, b, dims=((1,), (0,))):
    return lax.dot_general(a, b, (dims, ((), ())), preferred_element_type=f32)


def split(x):
    hi = x.astype(bf16)
    return hi, (x - hi.astype(f32)).astype(bf16)


def pairs(hi, lo):
    row = jnp.concatenate([hi, lo], axis=1)
    return row, jnp.concatenate([row, row], axis=0)


def halves(r):
    return r[:, :BLK] + r[:, BLK:]


def newton(covs):
    i = lax.broadcasted_iota(jnp.int32, (BLK, BLK), 0)
    j = lax.broadcasted_iota(jnp.int32, (BLK, BLK), 1)
    diag = i == j
    ts, xs, invs = [], [], []
    for c in covs:
        tr = jnp.sum(jnp.where(diag, c, 0.0), keepdims=True)
        m = c + jnp.where(diag, DAMPING * (tr / BLK), 0.0)
        inv = 1.0 / jnp.sum(jnp.where(diag, m, 0.0), keepdims=True)
        t = m * inv
        ts.append(t)
        xs.append(jnp.where(diag, 2.0, 0.0) - t)
        invs.append(inv)
    for step in range(ITERS):
        for b in range(len(covs)):
            t, x = ts[b], xs[b]
            t_row, t_mat = pairs(*split(t))
            if step == 0:
                ts[b] = 2.0 * t - halves(dot(t_row, t_mat))
                continue
            x_row = jnp.concatenate(split(x), axis=1)
            if step == ITERS - 1:
                xs[b] = 2.0 * x - halves(dot(x_row, t_mat))
                continue
            r = halves(dot(jnp.concatenate([t_row, x_row], axis=0), t_mat))
            ts[b] = 2.0 * t - r[:BLK]
            xs[b] = 2.0 * x - r[BLK:]
    return [x * inv for x, inv in zip(xs, invs)]


def kernel(n_dp, n_inv, cap, acts_t, grads, pos_col, pos_row, w_row, count, out,
           acts_all, place, pa, fl, fr, own, q, stage,
           a_send, a_recv, l_send, l_recv, r_send, r_recv, o_sem):
    dp = lax.axis_index("dp")
    z = lax.axis_index("inv")
    units = acts_t.shape[0]
    tp = grads.shape[0]
    chunks, live, width = own.shape
    tokens = pos_col.shape[0]

    barrier = pltpu.get_barrier_semaphore()

    def greet(d, _):
        pl.semaphore_signal(barrier, inc=1, device_id={"dp": lax.rem(dp + d, n_dp)}, device_id_type=MESH)
        return 0

    lax.fori_loop(1, n_dp, greet, 0)

    @pl.when(z > 0)
    def _():
        pl.semaphore_signal(barrier, inc=1, device_id={"inv": z - 1}, device_id_type=MESH)

    @pl.when(z < n_inv - 1)
    def _():
        pl.semaphore_signal(barrier, inc=1, device_id={"inv": z + 1}, device_id_type=MESH)

    at_end = (z == 0) | (z == n_inv - 1)

    @pl.when(at_end)
    def _():
        pl.semaphore_wait(barrier, n_dp)

    @pl.when(jnp.logical_not(at_end))
    def _():
        pl.semaphore_wait(barrier, n_dp + 1)

    def acts_copy(owner, peer):
        cols = pl.ds(pl.multiple_of(owner * TOK_DEV, TOK_DEV), TOK_DEV)
        return pltpu.make_async_remote_copy(
            src_ref=acts_t, dst_ref=acts_all.at[:, cols], send_sem=a_send.at[peer], recv_sem=a_recv.at[owner],
            device_id={"dp": peer}, device_id_type=MESH)

    def send_acts(d, _):
        acts_copy(dp, lax.rem(dp + d, n_dp)).start()
        return 0

    lax.fori_loop(1, n_dp, send_acts, 0)

    def wait_acts(d, _):
        peer = lax.rem(dp + d, n_dp)
        acts_copy(peer, peer).wait_recv()
        return 0

    def wait_acts_sent(d, _):
        acts_copy(dp, lax.rem(dp + d, n_dp)).wait_send()
        return 0

    hops = min(-(-cap // tp), n_inv - 1)
    left_rows = []
    right_rows = []
    for k in range(hops):
        hi = live - k * tp
        lo = max(live - cap, hi - tp)
        left_rows.append((lo, hi - lo))
        right_rows.append((k * tp, min(cap, (k + 1) * tp) - k * tp))

    def left_copy(c, k):
        lo, size = left_rows[k]
        part = fr.at[c, pl.ds(lo, size), :]
        return pltpu.make_async_remote_copy(
            src_ref=part, dst_ref=part, send_sem=l_send.at[k, c], recv_sem=l_recv.at[k, c],
            device_id={"inv": lax.max(z - 1, 0)}, device_id_type=MESH)

    def right_copy(c, k):
        lo, size = right_rows[k]
        part = fl.at[c, pl.ds(lo, size), :]
        return pltpu.make_async_remote_copy(
            src_ref=part, dst_ref=part, send_sem=r_send.at[k, c], recv_sem=r_recv.at[k, c],
            device_id={"inv": lax.min(z + 1, n_inv - 1)}, device_id_type=MESH)

    def leftward(c):
        if cap < live:
            fr[c, :live - cap, :] = own[c, :live - cap, :]
        for k in range(hops):
            lo, size = left_rows[k]
            rows = pl.ds(lo, size)

            @pl.when(z < n_inv - 1 - k)
            def _():
                left_copy(c, k).wait_recv()
                fr[c, rows, :] = fr[c, rows, :] + own[c, rows, :]

            @pl.when(z >= n_inv - 1 - k)
            def _():
                fr[c, rows, :] = own[c, rows, :]

            @pl.when((z > 0) & (z < n_inv - k))
            def _():
                left_copy(c, k).start()

    def rightward(c):
        if cap < live:
            fl[c, cap:, :] = own[c, cap:, :]
        for k in range(hops):
            lo, size = right_rows[k]
            rows = pl.ds(lo, size)

            @pl.when(z > k)
            def _():
                right_copy(c, k).wait_recv()
                fl[c, rows, :] = fl[c, rows, :] + own[c, rows, :]

            @pl.when(z <= k)
            def _():
                fl[c, rows, :] = own[c, rows, :]

            @pl.when((z < n_inv - 1) & (z >= k))
            def _():
                right_copy(c, k).start()

    slot = lax.broadcasted_iota(jnp.int32, (live, tp), 0)
    place_own = jnp.where(slot == pos_row[...], w_row[...], 0.0).astype(bf16)

    def relay(c, _):
        cols = pl.ds(pl.multiple_of(c * width, width), width)
        own[c] = dot(place_own, grads[:, cols]).astype(bf16)

        @pl.when(z >= n_inv // 2)
        def _():
            leftward(c)

        @pl.when(z < n_inv - 1)
        def _():
            rightward(c)

        @pl.when((z > 0) & (z < n_inv // 2))
        def _():
            leftward(c)

        return 0

    def merge(c):
        @pl.when(z == 0)
        def _():
            leftward(c)

        @pl.when(z == n_inv - 1)
        def _():
            rightward(c)

        both = fr[c].astype(f32) + fl[c].astype(f32)
        own[c] = (both - own[c].astype(f32)).astype(bf16)

    pair = 2 if chunks % 2 == 0 else 1
    early = min(2, chunks // pair)

    def output_side(p, _):
        spots = [(p * pair + i // (width // BLK), i % (width // BLK)) for i in range(pair * width // BLK)]
        for i in range(pair):
            merge(p * pair + i)
        parts = [own[c, :, j * BLK:(j + 1) * BLK] for c, j in spots]
        covs = [dot(s, s, ((0,), (0,))) for s in parts]
        for (c, j), s, x in zip(spots, parts, newton(covs)):
            hi, lo = split(halves(dot(s, jnp.concatenate(split(x), axis=1))))
            cols = slice(j * BLK, (j + 1) * BLK)
            q[c, :live, cols] = hi
            q[c, live:2 * live, cols] = hi
            q[c, 2 * live:, cols] = lo
        return 0

    done = 0
    for p, more in ((0, 4), (1, 3)):
        if p < early:
            lax.fori_loop(done, min(done + more, chunks), relay, 0)
            done = min(done + more, chunks)
            output_side(p, 0)
    lax.fori_loop(done, min(done + 2, chunks), relay, 0)
    done = min(done + 2, chunks)

    acts_all[:, pl.ds(pl.multiple_of(dp * TOK_DEV, TOK_DEV), TOK_DEV)] = acts_t[...]
    lax.fori_loop(1, n_dp, wait_acts, 0)
    step_rows = 512 if units % 512 == 0 else units
    piece = place.shape[0]
    for at in range(0, tokens, piece):
        def fill(s, _):
            rows = pl.ds(pl.multiple_of(s * TOK_DEV, TOK_DEV), TOK_DEV)
            ids = pl.ds(pl.multiple_of(at + s * TOK_DEV, TOK_DEV), TOK_DEV)
            spot = lax.broadcasted_iota(jnp.int32, (TOK_DEV, live), 1)
            place[rows, :] = jnp.where(spot == pos_col[ids, :], 1.0, 0.0).astype(bf16)
            return 0

        lax.fori_loop(0, piece // TOK_DEV, fill, 0)

        def put(m, _):
            rows = pl.ds(pl.multiple_of(m * step_rows, step_rows), step_rows)
            r = dot(acts_all[rows, at:at + piece], place[...]).astype(bf16)
            pa[rows, 2 * live:] = r if at == 0 else pa[rows, 2 * live:] + r
            return 0

        lax.fori_loop(0, units // step_rows, put, 0)

    a_blocks = units // BLK
    group = max(g for g in (1, 2, 3, 4) if a_blocks % g == 0)

    def input_side(g, _):
        rows = [pl.ds(pl.multiple_of((g * group + i) * BLK, BLK), BLK) for i in range(group)]
        masked = [pa[r, 2 * live:] for r in rows]
        covs = [dot(m, m, ((1,), (1,))) for m in masked]
        for r, m, x in zip(rows, masked, newton(covs)):
            x_row = jnp.concatenate(split(x * count[...]), axis=1)
            hi, lo = split(dot(x_row, jnp.concatenate([m, m], axis=0)))
            pa[r, :live] = hi
            pa[r, live:2 * live] = lo
            pa[r, 2 * live:] = hi

        @pl.when(done + g < chunks)
        def _():
            relay(done + g, 0)

        return 0

    lax.fori_loop(0, a_blocks // group, input_side, 0)
    lax.fori_loop(min(done + a_blocks // group, chunks), chunks, relay, 0)

    def out_copy(c):
        cols = pl.ds(pl.multiple_of(c * width, width), width)
        return pltpu.make_async_copy(stage.at[c], out.at[:, cols], o_sem.at[c])

    def finish(c, _):
        def rows_step(m, _):
            rows = pl.ds(pl.multiple_of(m * step_rows, step_rows), step_rows)
            stage[c, rows, :] = dot(pa[rows, :], q[c]).astype(bf16)
            return 0

        lax.fori_loop(0, units // step_rows, rows_step, 0)
        out_copy(c).start()
        return 0

    lax.fori_loop(0, early * pair, finish, 0)

    def main(p, _):
        output_side(p, 0)
        lax.fori_loop(p * pair, p * pair + pair, finish, 0)
        return 0

    lax.fori_loop(early, chunks // pair, main, 0)

    lax.fori_loop(1, n_dp, wait_acts_sent, 0)

    def drain(c, _):
        out_copy(c).wait()
        for k in range(hops):
            @pl.when((z > 0) & (z < n_inv - k))
            def _():
                left_copy(c, k).wait_send()

            @pl.when((z < n_inv - 1) & (z >= k))
            def _():
                right_copy(c, k).wait_send()
        return 0

    lax.fori_loop(0, chunks, drain, 0)


def call(n_dp, n_inv, cap, collective_id, acts_t, grads, pos_col, pos_row, w_row, count):
    units, tp, cols = acts_t.shape[0], grads.shape[0], grads.shape[1]
    tokens = pos_col.shape[0]
    live = tokens * 3 // 4
    chunks = cols // WIDTH
    hops = min(-(-cap // tp), n_inv - 1)
    vmem = pl.BlockSpec(memory_space=pltpu.VMEM)
    return pl.pallas_call(
        functools.partial(kernel, n_dp, n_inv, cap),
        out_shape=jax.ShapeDtypeStruct((units, cols), bf16),
        in_specs=[vmem] * 6,
        out_specs=pl.BlockSpec(memory_space=pl.ANY),
        scratch_shapes=[
            pltpu.VMEM((units, tokens), bf16),
            pltpu.VMEM((min(tokens, 1024), live), bf16),
            pltpu.VMEM((units, 3 * live), bf16),
            pltpu.VMEM((chunks, live, WIDTH), bf16),
            pltpu.VMEM((chunks, live, WIDTH), bf16),
            pltpu.VMEM((chunks, live, WIDTH), bf16),
            pltpu.VMEM((chunks, 3 * live, WIDTH), bf16),
            pltpu.VMEM((chunks, units, WIDTH), bf16),
            pltpu.SemaphoreType.DMA((n_dp,)),
            pltpu.SemaphoreType.DMA((n_dp,)),
            pltpu.SemaphoreType.DMA((hops, chunks)),
            pltpu.SemaphoreType.DMA((hops, chunks)),
            pltpu.SemaphoreType.DMA((hops, chunks)),
            pltpu.SemaphoreType.DMA((hops, chunks)),
            pltpu.SemaphoreType.DMA((chunks,)),
        ],
        compiler_params=pltpu.CompilerParams(
            collective_id=collective_id, has_side_effects=True, vmem_limit_bytes=60 * 2**20),
        cost_estimate=pl.CostEstimate(
            flops=6 * units * live * cols, bytes_accessed=4 * units * cols, transcendentals=0),
    )(acts_t, grads, pos_col, pos_row, w_row, count)


def local(n_dp, n_inv, acts, grads_out, scale_exp, shard_tokens):
    tp = grads_out.shape[0]
    tokens = acts.shape[0] * n_dp
    ids = jnp.arange(tokens, dtype=jnp.int32)
    in_shard = ids % TOK_DEV
    limit = jnp.repeat(shard_tokens, TOK_DEV)
    first = jnp.repeat(jnp.cumsum(shard_tokens) - shard_tokens, TOK_DEV)
    pos = jnp.where(in_shard < limit, first + in_shard, -1).astype(jnp.int32)
    weight = jnp.exp2(-scale_exp.astype(f32))
    start = lax.axis_index("inv") * tp
    pos_row = lax.dynamic_slice_in_dim(pos, start, tp)[None, :]
    w_row = lax.dynamic_slice_in_dim(weight, start, tp)[None, :]
    count = jnp.sum(shard_tokens).astype(f32).reshape(1, 1)
    live = tokens * 3 // 4
    return call(n_dp, n_inv, live, 0, acts.T, grads_out, pos[:, None], pos_row, w_row, count)


def solution(mesh):
    placed = (P("dp", "inv"), P("inv", "dp"), P(), P())
    return jax.shard_map(
        functools.partial(local, mesh.shape["dp"], mesh.shape["inv"]),
        mesh=mesh, in_specs=placed, out_specs=P("inv", "dp"), check_vma=False)
```

```python
import functools

import jax
import jax.numpy as jnp
from jax import lax
from jax.experimental import pallas as pl
from jax.experimental.pallas import tpu as pltpu
from jax.sharding import PartitionSpec as P

BLK = 128
ITERS = 8
TOK_DEV = 128
WIDTH = 256
DAMPING = 0.001
MESH = pl.DeviceIdType.MESH
f32, bf16 = jnp.float32, jnp.bfloat16


def dot(a, b, dims=((1,), (0,))):
    return lax.dot_general(a, b, (dims, ((), ())), preferred_element_type=f32)


def split(x):
    hi = x.astype(bf16)
    return hi, (x - hi.astype(f32)).astype(bf16)


def pairs(hi, lo):
    row = jnp.concatenate([hi, lo], axis=1)
    return row, jnp.concatenate([row, row], axis=0)


def halves(r):
    return r[:, :BLK] + r[:, BLK:]


def newton(covs):
    i = lax.broadcasted_iota(jnp.int32, (BLK, BLK), 0)
    j = lax.broadcasted_iota(jnp.int32, (BLK, BLK), 1)
    diag = i == j
    ts, xs, invs = [], [], []
    for c in covs:
        tr = jnp.sum(jnp.where(diag, c, 0.0), keepdims=True)
        m = c + jnp.where(diag, DAMPING * (tr / BLK), 0.0)
        inv = 1.0 / jnp.sum(jnp.where(diag, m, 0.0), keepdims=True)
        t = m * inv
        ts.append(t)
        xs.append(jnp.where(diag, 2.0, 0.0) - t)
        invs.append(inv)
    for step in range(ITERS):
        for b in range(len(covs)):
            t, x = ts[b], xs[b]
            t_row, t_mat = pairs(*split(t))
            if step == 0:
                ts[b] = 2.0 * t - halves(dot(t_row, t_mat))
                continue
            x_row = jnp.concatenate(split(x), axis=1)
            if step == ITERS - 1:
                xs[b] = 2.0 * x - halves(dot(x_row, t_mat))
                continue
            r = halves(dot(jnp.concatenate([t_row, x_row], axis=0), t_mat))
            ts[b] = 2.0 * t - r[:BLK]
            xs[b] = 2.0 * x - r[BLK:]
    return [x * inv for x, inv in zip(xs, invs)]


def kernel(n_dp, n_inv, cap, acts_t, grads, pos_col, pos_row, exps, count, out,
           acts_all, place, pa, fl, fr, own, q, stage,
           a_send, a_recv, l_send, l_recv, r_send, r_recv, o_sem):
    dp = lax.axis_index("dp")
    z = lax.axis_index("inv")
    units = acts_t.shape[0]
    tp = grads.shape[0]
    chunks, live, width = own.shape
    tokens = pos_col.shape[0]

    barrier = pltpu.get_barrier_semaphore()

    def greet(d, _):
        pl.semaphore_signal(barrier, inc=1, device_id={"dp": lax.rem(dp + d, n_dp)}, device_id_type=MESH)
        return 0

    lax.fori_loop(1, n_dp, greet, 0)

    @pl.when(z > 0)
    def _():
        pl.semaphore_signal(barrier, inc=1, device_id={"inv": z - 1}, device_id_type=MESH)

    @pl.when(z < n_inv - 1)
    def _():
        pl.semaphore_signal(barrier, inc=1, device_id={"inv": z + 1}, device_id_type=MESH)

    at_end = (z == 0) | (z == n_inv - 1)

    @pl.when(at_end)
    def _():
        pl.semaphore_wait(barrier, n_dp)

    @pl.when(jnp.logical_not(at_end))
    def _():
        pl.semaphore_wait(barrier, n_dp + 1)

    def acts_copy(owner, peer):
        cols = pl.ds(pl.multiple_of(owner * TOK_DEV, TOK_DEV), TOK_DEV)
        return pltpu.make_async_remote_copy(
            src_ref=acts_t, dst_ref=acts_all.at[:, cols], send_sem=a_send.at[peer], recv_sem=a_recv.at[owner],
            device_id={"dp": peer}, device_id_type=MESH)

    def send_acts(d, _):
        acts_copy(dp, lax.rem(dp + d, n_dp)).start()
        return 0

    lax.fori_loop(1, n_dp, send_acts, 0)

    def wait_acts(d, _):
        peer = lax.rem(dp + d, n_dp)
        acts_copy(peer, peer).wait_recv()
        return 0

    def wait_acts_sent(d, _):
        acts_copy(dp, lax.rem(dp + d, n_dp)).wait_send()
        return 0

    hops = min(-(-cap // tp), n_inv - 1)
    left_rows = []
    right_rows = []
    for k in range(hops):
        hi = live - k * tp
        lo = max(live - cap, hi - tp)
        left_rows.append((lo, hi - lo))
        right_rows.append((k * tp, min(cap, (k + 1) * tp) - k * tp))

    def left_copy(c, k):
        lo, size = left_rows[k]
        part = fr.at[c, pl.ds(lo, size), :]
        return pltpu.make_async_remote_copy(
            src_ref=part, dst_ref=part, send_sem=l_send.at[k, c], recv_sem=l_recv.at[k, c],
            device_id={"inv": lax.max(z - 1, 0)}, device_id_type=MESH)

    def right_copy(c, k):
        lo, size = right_rows[k]
        part = fl.at[c, pl.ds(lo, size), :]
        return pltpu.make_async_remote_copy(
            src_ref=part, dst_ref=part, send_sem=r_send.at[k, c], recv_sem=r_recv.at[k, c],
            device_id={"inv": lax.min(z + 1, n_inv - 1)}, device_id_type=MESH)

    def leftward(c):
        if cap < live:
            fr[c, :live - cap, :] = own[c, :live - cap, :]
        for k in range(hops):
            lo, size = left_rows[k]
            rows = pl.ds(lo, size)

            @pl.when(z < n_inv - 1 - k)
            def _():
                left_copy(c, k).wait_recv()
                fr[c, rows, :] = fr[c, rows, :] + own[c, rows, :]

            @pl.when(z >= n_inv - 1 - k)
            def _():
                fr[c, rows, :] = own[c, rows, :]

            @pl.when((z > 0) & (z < n_inv - k))
            def _():
                left_copy(c, k).start()

    def rightward(c):
        if cap < live:
            fl[c, cap:, :] = own[c, cap:, :]
        for k in range(hops):
            lo, size = right_rows[k]
            rows = pl.ds(lo, size)

            @pl.when(z > k)
            def _():
                right_copy(c, k).wait_recv()
                fl[c, rows, :] = fl[c, rows, :] + own[c, rows, :]

            @pl.when(z <= k)
            def _():
                fl[c, rows, :] = own[c, rows, :]

            @pl.when((z < n_inv - 1) & (z >= k))
            def _():
                right_copy(c, k).start()

    slot = lax.broadcasted_iota(jnp.int32, (live, tp), 0)
    mine = pl.ds(pl.multiple_of(z * tp, TOK_DEV), tp)
    e = exps[:, mine]
    weight = jnp.where(e == 0, 1.0, jnp.where(e == 1, 0.5, jnp.where(e == 2, 0.25, 0.125)))
    place_own = jnp.where(slot == pos_row[:, mine], weight, 0.0).astype(bf16)

    def near(c, _):
        cols = pl.ds(pl.multiple_of(c * width, width), width)
        own[c] = dot(place_own, grads[:, cols]).astype(bf16)

        @pl.when(z >= n_inv // 2)
        def _():
            leftward(c)

        @pl.when(z < n_inv // 2)
        def _():
            rightward(c)

        return 0

    def far(c, _):
        @pl.when((z >= n_inv // 2) & (z < n_inv - 1))
        def _():
            rightward(c)

        @pl.when((z < n_inv // 2) & (z > 0))
        def _():
            leftward(c)

        return 0

    at = {"near": 0, "far": 0}

    def advance(nears, fars):
        to = min(at["near"] + nears, chunks)
        lax.fori_loop(at["near"], to, near, 0)
        at["near"] = to
        to = min(at["far"] + fars, to)
        lax.fori_loop(at["far"], to, far, 0)
        at["far"] = to

    def merge(c):
        @pl.when(z == 0)
        def _():
            leftward(c)

        @pl.when(z == n_inv - 1)
        def _():
            rightward(c)

        both = fr[c].astype(f32) + fl[c].astype(f32)
        own[c] = (both - own[c].astype(f32)).astype(bf16)

    pair = 2 if chunks % 2 == 0 else 1
    early = min(2, chunks // pair)

    def output_side(p, _):
        spots = [(p * pair + i // (width // BLK), i % (width // BLK)) for i in range(pair * width // BLK)]
        for i in range(pair):
            merge(p * pair + i)
        parts = [own[c, :, j * BLK:(j + 1) * BLK] for c, j in spots]
        covs = [dot(s, s, ((0,), (0,))) for s in parts]
        for (c, j), s, x in zip(spots, parts, newton(covs)):
            hi, lo = split(halves(dot(s, jnp.concatenate(split(x), axis=1))))
            cols = slice(j * BLK, (j + 1) * BLK)
            q[c, :live, cols] = hi
            q[c, live:2 * live, cols] = hi
            q[c, 2 * live:, cols] = lo
        return 0

    advance(4, 2)
    for p, (nears, fars) in enumerate(((2, 0), (2, 3))):
        if p < early:
            advance(nears, max(fars, (p + 1) * pair - at["far"]))
            output_side(p, 0)
    advance(2, 3)
    near_done, far_done = at["near"], at["far"]

    acts_all[:, pl.ds(pl.multiple_of(dp * TOK_DEV, TOK_DEV), TOK_DEV)] = acts_t[...]
    lax.fori_loop(1, n_dp, wait_acts, 0)
    step_rows = 512 if units % 512 == 0 else units
    piece = place.shape[0]
    for base in range(0, tokens, piece):
        def fill(s, _):
            rows = pl.ds(pl.multiple_of(s * TOK_DEV, TOK_DEV), TOK_DEV)
            ids = pl.ds(pl.multiple_of(base + s * TOK_DEV, TOK_DEV), TOK_DEV)
            spot = lax.broadcasted_iota(jnp.int32, (TOK_DEV, live), 1)
            place[rows, :] = jnp.where(spot == pos_col[ids, :], 1.0, 0.0).astype(bf16)
            return 0

        lax.fori_loop(0, piece // TOK_DEV, fill, 0)

        def put(m, _):
            rows = pl.ds(pl.multiple_of(m * step_rows, step_rows), step_rows)
            r = dot(acts_all[rows, base:base + piece], place[...]).astype(bf16)
            pa[rows, 2 * live:] = r if base == 0 else pa[rows, 2 * live:] + r
            return 0

        lax.fori_loop(0, units // step_rows, put, 0)

    a_blocks = units // BLK
    group = max(g for g in (1, 2, 3, 4) if a_blocks % g == 0)

    def input_side(g, _):
        rows = [pl.ds(pl.multiple_of((g * group + i) * BLK, BLK), BLK) for i in range(group)]
        masked = [pa[r, 2 * live:] for r in rows]
        covs = [dot(m, m, ((1,), (1,))) for m in masked]
        for r, m, x in zip(rows, masked, newton(covs)):
            x_row = jnp.concatenate(split(x * count[...]), axis=1)
            hi, lo = split(dot(x_row, jnp.concatenate([m, m], axis=0)))
            pa[r, :live] = hi
            pa[r, live:2 * live] = lo
            pa[r, 2 * live:] = hi

        @pl.when(near_done + g < chunks)
        def _():
            near(near_done + g, 0)

        @pl.when(far_done + g < chunks)
        def _():
            far(far_done + g, 0)

        return 0

    groups = a_blocks // group
    lax.fori_loop(0, groups, input_side, 0)
    lax.fori_loop(min(near_done + groups, chunks), chunks, near, 0)
    lax.fori_loop(min(far_done + groups, chunks), chunks, far, 0)

    def out_copy(c):
        cols = pl.ds(pl.multiple_of(c * width, width), width)
        return pltpu.make_async_copy(stage.at[c], out.at[:, cols], o_sem.at[c])

    def finish(c, _):
        def rows_step(m, _):
            rows = pl.ds(pl.multiple_of(m * step_rows, step_rows), step_rows)
            stage[c, rows, :] = dot(pa[rows, :], q[c]).astype(bf16)
            return 0

        lax.fori_loop(0, units // step_rows, rows_step, 0)
        out_copy(c).start()
        return 0

    lax.fori_loop(0, early * pair, finish, 0)

    def main(p, _):
        output_side(p, 0)
        lax.fori_loop(p * pair, p * pair + pair, finish, 0)
        return 0

    lax.fori_loop(early, chunks // pair, main, 0)

    lax.fori_loop(1, n_dp, wait_acts_sent, 0)

    def drain(c, _):
        out_copy(c).wait()
        for k in range(hops):
            @pl.when((z > 0) & (z < n_inv - k))
            def _():
                left_copy(c, k).wait_send()

            @pl.when((z < n_inv - 1) & (z >= k))
            def _():
                right_copy(c, k).wait_send()
        return 0

    lax.fori_loop(0, chunks, drain, 0)


def call(n_dp, n_inv, cap, collective_id, acts_t, grads, pos_col, pos_row, exps, count):
    units, tp, cols = acts_t.shape[0], grads.shape[0], grads.shape[1]
    tokens = pos_col.shape[0]
    live = tokens * 3 // 4
    chunks = cols // WIDTH
    hops = min(-(-cap // tp), n_inv - 1)
    vmem = pl.BlockSpec(memory_space=pltpu.VMEM)
    return pl.pallas_call(
        functools.partial(kernel, n_dp, n_inv, cap),
        out_shape=jax.ShapeDtypeStruct((units, cols), bf16),
        in_specs=[vmem] * 6,
        out_specs=pl.BlockSpec(memory_space=pl.ANY),
        scratch_shapes=[
            pltpu.VMEM((units, tokens), bf16),
            pltpu.VMEM((min(tokens, 1024), live), bf16),
            pltpu.VMEM((units, 3 * live), bf16),
            pltpu.VMEM((chunks, live, WIDTH), bf16),
            pltpu.VMEM((chunks, live, WIDTH), bf16),
            pltpu.VMEM((chunks, live, WIDTH), bf16),
            pltpu.VMEM((chunks, 3 * live, WIDTH), bf16),
            pltpu.VMEM((chunks, units, WIDTH), bf16),
            pltpu.SemaphoreType.DMA((n_dp,)),
            pltpu.SemaphoreType.DMA((n_dp,)),
            pltpu.SemaphoreType.DMA((hops, chunks)),
            pltpu.SemaphoreType.DMA((hops, chunks)),
            pltpu.SemaphoreType.DMA((hops, chunks)),
            pltpu.SemaphoreType.DMA((hops, chunks)),
            pltpu.SemaphoreType.DMA((chunks,)),
        ],
        compiler_params=pltpu.CompilerParams(
            collective_id=collective_id, has_side_effects=True, vmem_limit_bytes=60 * 2**20),
        cost_estimate=pl.CostEstimate(
            flops=6 * units * live * cols, bytes_accessed=4 * units * cols, transcendentals=0),
    )(acts_t, grads, pos_col, pos_row, exps, count)


def local(n_dp, n_inv, acts, grads_out, scale_exp, shard_tokens):
    tokens = acts.shape[0] * n_dp
    shards = tokens // TOK_DEV
    order = jnp.arange(shards)
    first = jnp.sum(jnp.where(order[None, :] < order[:, None], shard_tokens[None, :], 0), axis=1)
    spot = jnp.arange(TOK_DEV, dtype=jnp.int32)[None, :]
    pos = jnp.where(spot < shard_tokens[:, None], first[:, None] + spot, -1).astype(jnp.int32)
    count = jnp.sum(shard_tokens).astype(f32).reshape(1, 1)
    live = tokens * 3 // 4
    return call(n_dp, n_inv, live, 0, acts.T, grads_out, pos.reshape(tokens, 1), pos.reshape(1, tokens),
                scale_exp.reshape(1, tokens), count)


def solution(mesh):
    placed = (P("dp", "inv"), P("inv", "dp"), P(), P())
    return jax.shard_map(
        functools.partial(local, mesh.shape["dp"], mesh.shape["inv"]),
        mesh=mesh, in_specs=placed, out_specs=P("inv", "dp"), check_vma=False)
```

```python
import functools

import jax
import jax.numpy as jnp
from jax import lax
from jax.experimental import pallas as pl
from jax.experimental.pallas import tpu as pltpu
from jax.sharding import PartitionSpec as P

BLK = 128
ITERS = 8
TOK_DEV = 128
WIDTH = 256
DAMPING = 0.001
MESH = pl.DeviceIdType.MESH
f32, bf16 = jnp.float32, jnp.bfloat16


def dot(a, b, dims=((1,), (0,))):
    return lax.dot_general(a, b, (dims, ((), ())), preferred_element_type=f32)


def split(x):
    hi = x.astype(bf16)
    return hi, (x - hi.astype(f32)).astype(bf16)


def pairs(hi, lo):
    row = jnp.concatenate([hi, lo], axis=1)
    return row, jnp.concatenate([row, row], axis=0)


def halves(r):
    return r[:, :BLK] + r[:, BLK:]


def newton(covs):
    i = lax.broadcasted_iota(jnp.int32, (BLK, BLK), 0)
    j = lax.broadcasted_iota(jnp.int32, (BLK, BLK), 1)
    diag = i == j
    ts, xs, invs = [], [], []
    for c in covs:
        tr = jnp.sum(jnp.where(diag, c, 0.0), keepdims=True)
        m = c + jnp.where(diag, DAMPING * (tr / BLK), 0.0)
        inv = 1.0 / jnp.sum(jnp.where(diag, m, 0.0), keepdims=True)
        t = m * inv
        ts.append(t)
        xs.append(jnp.where(diag, 2.0, 0.0) - t)
        invs.append(inv)
    for step in range(ITERS):
        for b in range(len(covs)):
            t, x = ts[b], xs[b]
            t_row, t_mat = pairs(*split(t))
            if step == 0:
                ts[b] = 2.0 * t - halves(dot(t_row, t_mat))
                continue
            x_row = jnp.concatenate(split(x), axis=1)
            if step == ITERS - 1:
                xs[b] = 2.0 * x - halves(dot(x_row, t_mat))
                continue
            r = halves(dot(jnp.concatenate([t_row, x_row], axis=0), t_mat))
            ts[b] = 2.0 * t - r[:BLK]
            xs[b] = 2.0 * x - r[BLK:]
    return [x * inv for x, inv in zip(xs, invs)]


def kernel(n_dp, n_inv, cap, acts_t, grads, pos_col, pos_row, exps, count, out,
           acts_all, place, pa, fl, fr, own, q, stage,
           a_send, a_recv, l_send, l_recv, r_send, r_recv, o_sem):
    dp = lax.axis_index("dp")
    z = lax.axis_index("inv")
    units = acts_t.shape[0]
    tp = grads.shape[0]
    chunks, live, width = own.shape
    tokens = pos_col.shape[0]

    barrier = pltpu.get_barrier_semaphore()

    def greet(d, _):
        pl.semaphore_signal(barrier, inc=1, device_id={"dp": lax.rem(dp + d, n_dp)}, device_id_type=MESH)
        return 0

    lax.fori_loop(1, n_dp, greet, 0)

    @pl.when(z > 0)
    def _():
        pl.semaphore_signal(barrier, inc=1, device_id={"inv": z - 1}, device_id_type=MESH)

    @pl.when(z < n_inv - 1)
    def _():
        pl.semaphore_signal(barrier, inc=1, device_id={"inv": z + 1}, device_id_type=MESH)

    at_end = (z == 0) | (z == n_inv - 1)

    @pl.when(at_end)
    def _():
        pl.semaphore_wait(barrier, n_dp)

    @pl.when(jnp.logical_not(at_end))
    def _():
        pl.semaphore_wait(barrier, n_dp + 1)

    def acts_copy(owner, peer):
        cols = pl.ds(pl.multiple_of(owner * TOK_DEV, TOK_DEV), TOK_DEV)
        return pltpu.make_async_remote_copy(
            src_ref=acts_t, dst_ref=acts_all.at[:, cols], send_sem=a_send.at[peer], recv_sem=a_recv.at[owner],
            device_id={"dp": peer}, device_id_type=MESH)

    def send_acts(d, _):
        acts_copy(dp, lax.rem(dp + d, n_dp)).start()
        return 0

    lax.fori_loop(1, n_dp, send_acts, 0)

    def wait_acts(d, _):
        peer = lax.rem(dp + d, n_dp)
        acts_copy(peer, peer).wait_recv()
        return 0

    def wait_acts_sent(d, _):
        acts_copy(dp, lax.rem(dp + d, n_dp)).wait_send()
        return 0

    hops = min(-(-cap // tp), n_inv - 1)
    left_rows = []
    right_rows = []
    for k in range(hops):
        hi = live - k * tp
        lo = max(live - cap, hi - tp)
        left_rows.append((lo, hi - lo))
        right_rows.append((k * tp, min(cap, (k + 1) * tp) - k * tp))

    def left_copy(c, k):
        lo, size = left_rows[k]
        part = fr.at[c, pl.ds(lo, size), :]
        return pltpu.make_async_remote_copy(
            src_ref=part, dst_ref=part, send_sem=l_send.at[k, c], recv_sem=l_recv.at[k, c],
            device_id={"inv": lax.max(z - 1, 0)}, device_id_type=MESH)

    def right_copy(c, k):
        lo, size = right_rows[k]
        part = fl.at[c, pl.ds(lo, size), :]
        return pltpu.make_async_remote_copy(
            src_ref=part, dst_ref=part, send_sem=r_send.at[k, c], recv_sem=r_recv.at[k, c],
            device_id={"inv": lax.min(z + 1, n_inv - 1)}, device_id_type=MESH)

    def leftward(c):
        if cap < live:
            fr[c, :live - cap, :] = own[c, :live - cap, :]
        for k in range(hops):
            lo, size = left_rows[k]
            rows = pl.ds(lo, size)

            @pl.when(z < n_inv - 1 - k)
            def _():
                left_copy(c, k).wait_recv()
                fr[c, rows, :] = fr[c, rows, :] + own[c, rows, :]

            @pl.when(z >= n_inv - 1 - k)
            def _():
                fr[c, rows, :] = own[c, rows, :]

            @pl.when((z > 0) & (z < n_inv - k))
            def _():
                left_copy(c, k).start()

    def rightward(c):
        if cap < live:
            fl[c, cap:, :] = own[c, cap:, :]
        for k in range(hops):
            lo, size = right_rows[k]
            rows = pl.ds(lo, size)

            @pl.when(z > k)
            def _():
                right_copy(c, k).wait_recv()
                fl[c, rows, :] = fl[c, rows, :] + own[c, rows, :]

            @pl.when(z <= k)
            def _():
                fl[c, rows, :] = own[c, rows, :]

            @pl.when((z < n_inv - 1) & (z >= k))
            def _():
                right_copy(c, k).start()

    slot = lax.broadcasted_iota(jnp.int32, (live, tp), 0)
    mine = pl.ds(pl.multiple_of(z * tp, TOK_DEV), tp)
    e = exps[:, mine]
    weight = jnp.where(e == 0, 1.0, jnp.where(e == 1, 0.5, jnp.where(e == 2, 0.25, 0.125)))
    place_own = jnp.where(slot == pos_row[:, mine], weight, 0.0).astype(bf16)

    def near(c, _):
        cols = pl.ds(pl.multiple_of(c * width, width), width)
        own[c] = dot(place_own, grads[:, cols]).astype(bf16)

        @pl.when(z >= n_inv // 2)
        def _():
            leftward(c)

        @pl.when(z < n_inv // 2)
        def _():
            rightward(c)

        return 0

    def far(c, _):
        @pl.when((z >= n_inv // 2) & (z < n_inv - 1))
        def _():
            rightward(c)

        @pl.when((z < n_inv // 2) & (z > 0))
        def _():
            leftward(c)

        return 0

    at = {"near": 0, "far": 0}

    def advance(nears, fars):
        to = min(at["near"] + nears, chunks)
        lax.fori_loop(at["near"], to, near, 0)
        at["near"] = to
        to = min(at["far"] + fars, to)
        lax.fori_loop(at["far"], to, far, 0)
        at["far"] = to

    def merge(c):
        @pl.when(z == 0)
        def _():
            leftward(c)

        @pl.when(z == n_inv - 1)
        def _():
            rightward(c)

        both = fr[c].astype(f32) + fl[c].astype(f32)
        own[c] = (both - own[c].astype(f32)).astype(bf16)

    pair = 2 if chunks % 2 == 0 else 1
    early = min(2, chunks // pair)

    def output_side(p, _):
        spots = [(p * pair + i // (width // BLK), i % (width // BLK)) for i in range(pair * width // BLK)]
        for i in range(pair):
            merge(p * pair + i)
        parts = [own[c, :, j * BLK:(j + 1) * BLK] for c, j in spots]
        covs = [dot(s, s, ((0,), (0,))) for s in parts]
        for (c, j), s, x in zip(spots, parts, newton(covs)):
            hi, lo = split(halves(dot(s, jnp.concatenate(split(x), axis=1))))
            cols = slice(j * BLK, (j + 1) * BLK)
            q[c, :live, cols] = hi
            q[c, live:2 * live, cols] = hi
            q[c, 2 * live:, cols] = lo
        return 0

    advance(4, 2)
    for p, (nears, fars) in enumerate(((2, 0), (2, 3))):
        if p < early:
            advance(nears, max(fars, (p + 1) * pair - at["far"]))
            output_side(p, 0)
    advance(2, 3)
    near_done, far_done = at["near"], at["far"]

    acts_all[:, pl.ds(pl.multiple_of(dp * TOK_DEV, TOK_DEV), TOK_DEV)] = acts_t[...]
    lax.fori_loop(1, n_dp, wait_acts, 0)
    step_rows = 512 if units % 512 == 0 else units
    piece = place.shape[0]
    for base in range(0, tokens, piece):
        def fill(s, _):
            rows = pl.ds(pl.multiple_of(s * TOK_DEV, TOK_DEV), TOK_DEV)
            ids = pl.ds(pl.multiple_of(base + s * TOK_DEV, TOK_DEV), TOK_DEV)
            spot = lax.broadcasted_iota(jnp.int32, (TOK_DEV, live), 1)
            place[rows, :] = jnp.where(spot == pos_col[ids, :], 1.0, 0.0).astype(bf16)
            return 0

        lax.fori_loop(0, piece // TOK_DEV, fill, 0)

        def put(m, _):
            rows = pl.ds(pl.multiple_of(m * step_rows, step_rows), step_rows)
            r = dot(acts_all[rows, base:base + piece], place[...]).astype(bf16)
            pa[rows, 2 * live:] = r if base == 0 else pa[rows, 2 * live:] + r
            return 0

        lax.fori_loop(0, units // step_rows, put, 0)

    a_blocks = units // BLK
    group = max(g for g in (1, 2, 3, 4) if a_blocks % g == 0)

    def input_side(g, _):
        rows = [pl.ds(pl.multiple_of((g * group + i) * BLK, BLK), BLK) for i in range(group)]
        masked = [pa[r, 2 * live:] for r in rows]
        covs = [dot(m, m, ((1,), (1,))) for m in masked]
        for r, m, x in zip(rows, masked, newton(covs)):
            x_row = jnp.concatenate(split(x * count[...]), axis=1)
            hi, lo = split(dot(x_row, jnp.concatenate([m, m], axis=0)))
            pa[r, :live] = hi
            pa[r, live:2 * live] = lo
            pa[r, 2 * live:] = hi

        @pl.when(near_done + g < chunks)
        def _():
            near(near_done + g, 0)

        @pl.when(far_done + g < chunks)
        def _():
            far(far_done + g, 0)

        return 0

    groups = a_blocks // group
    lax.fori_loop(0, groups, input_side, 0)
    lax.fori_loop(min(near_done + groups, chunks), chunks, near, 0)
    lax.fori_loop(min(far_done + groups, chunks), chunks, far, 0)

    def out_copy(c):
        cols = pl.ds(pl.multiple_of(c * width, width), width)
        return pltpu.make_async_copy(stage.at[c], out.at[:, cols], o_sem.at[c])

    def finish(c, _):
        def rows_step(m, _):
            rows = pl.ds(pl.multiple_of(m * step_rows, step_rows), step_rows)
            stage[c, rows, :] = dot(pa[rows, :], q[c]).astype(bf16)
            return 0

        lax.fori_loop(0, units // step_rows, rows_step, 0)
        out_copy(c).start()
        return 0

    lax.fori_loop(0, early * pair, finish, 0)

    def main(p, _):
        output_side(p, 0)
        lax.fori_loop(p * pair, p * pair + pair, finish, 0)
        return 0

    lax.fori_loop(early, chunks // pair, main, 0)

    lax.fori_loop(1, n_dp, wait_acts_sent, 0)

    def drain(c, _):
        out_copy(c).wait()
        for k in range(hops):
            @pl.when((z > 0) & (z < n_inv - k))
            def _():
                left_copy(c, k).wait_send()

            @pl.when((z < n_inv - 1) & (z >= k))
            def _():
                right_copy(c, k).wait_send()
        return 0

    lax.fori_loop(0, chunks, drain, 0)


def call(n_dp, n_inv, cap, collective_id, acts_t, grads, pos_col, pos_row, exps, count):
    units, tp, cols = acts_t.shape[0], grads.shape[0], grads.shape[1]
    tokens = pos_col.shape[0]
    live = tokens * 3 // 4
    chunks = cols // WIDTH
    hops = min(-(-cap // tp), n_inv - 1)
    vmem = pl.BlockSpec(memory_space=pltpu.VMEM)
    return pl.pallas_call(
        functools.partial(kernel, n_dp, n_inv, cap),
        out_shape=jax.ShapeDtypeStruct((units, cols), bf16),
        in_specs=[vmem] * 6,
        out_specs=pl.BlockSpec(memory_space=pl.ANY),
        scratch_shapes=[
            pltpu.VMEM((units, tokens), bf16),
            pltpu.VMEM((min(tokens, 1024), live), bf16),
            pltpu.VMEM((units, 3 * live), bf16),
            pltpu.VMEM((chunks, live, WIDTH), bf16),
            pltpu.VMEM((chunks, live, WIDTH), bf16),
            pltpu.VMEM((chunks, live, WIDTH), bf16),
            pltpu.VMEM((chunks, 3 * live, WIDTH), bf16),
            pltpu.VMEM((chunks, units, WIDTH), bf16),
            pltpu.SemaphoreType.DMA((n_dp,)),
            pltpu.SemaphoreType.DMA((n_dp,)),
            pltpu.SemaphoreType.DMA((hops, chunks)),
            pltpu.SemaphoreType.DMA((hops, chunks)),
            pltpu.SemaphoreType.DMA((hops, chunks)),
            pltpu.SemaphoreType.DMA((hops, chunks)),
            pltpu.SemaphoreType.DMA((chunks,)),
        ],
        compiler_params=pltpu.CompilerParams(
            collective_id=collective_id, has_side_effects=True, vmem_limit_bytes=60 * 2**20),
        cost_estimate=pl.CostEstimate(
            flops=6 * units * live * cols, bytes_accessed=4 * units * cols, transcendentals=0),
    )(acts_t, grads, pos_col, pos_row, exps, count)


def local(n_dp, n_inv, acts, grads_out, scale_exp, shard_tokens):
    tokens = acts.shape[0] * n_dp
    shards = tokens // TOK_DEV
    order = jnp.arange(shards)
    first = jnp.sum(jnp.where(order[None, :] < order[:, None], shard_tokens[None, :], 0), axis=1)
    spot = jnp.arange(TOK_DEV, dtype=jnp.int32)[None, :]
    pos = jnp.where(spot < shard_tokens[:, None], first[:, None] + spot, -1).astype(jnp.int32)
    count = jnp.sum(shard_tokens).astype(f32).reshape(1, 1)
    live = tokens * 3 // 4
    args = (acts.T, grads_out, pos.reshape(tokens, 1), pos.reshape(1, tokens), scale_exp.reshape(1, tokens), count)
    full = functools.partial(call, n_dp, n_inv, live, 0)
    tp = grads_out.shape[0]
    cap = live * 5 // 6
    if live - cap > tp:
        return full(*args)
    ends = shard_tokens.reshape(n_inv, tp // TOK_DEV).sum(axis=1)
    few = jnp.minimum(ends[0], ends[-1]) >= live - cap
    return lax.cond(few, functools.partial(call, n_dp, n_inv, cap, 1), full, *args)


def solution(mesh):
    placed = (P("dp", "inv"), P("inv", "dp"), P(), P())
    return jax.shard_map(
        functools.partial(local, mesh.shape["dp"], mesh.shape["inv"]),
        mesh=mesh, in_specs=placed, out_specs=P("inv", "dp"), check_vma=False)
```
